256 devices in a mesh: ex: 8 (over x, z_lo), feat: 32 (over z_hi, y, core).
Axes of the slice: x: 4, y: 4, z: 8 (z_hi: 4, z_lo: 2; z = z_hi * 2 + z_lo), core: 2. Of those that a mesh axis runs over, the one named last changes fastest.
Arguments:
- train_grads: bfloat16 [8192, 65536], P('ex', 'feat'), may hold values from -6 to 6
- queries: bfloat16 [1024, 65536], P(('ex', 'feat')), may hold values from -24 to 24
- inv_out: float32 [16, 64, 64], replicated, may hold values from -1 to 5
- inv_in: float32 [16, 64, 64], replicated, may hold values from -1 to 5
- module_rank: int32 [16], replicated, may hold values from 1 to 64, 768 in all
Outputs:
- scores: float32 [8192, 1024], P('ex', 'feat')
The draws below stay inside these ranges and needn't reach their ends.
Inputs may be any that keep to these rules, and one draw needn't show every extreme that they name: `module_rank`: some module has all 64 rows live.
All inputs are finite; a program needn't handle non-finite values.
Results may differ from the reference program's by a relative error of at most 0.0029.
Values may be sent and summed in bfloat16 or wider, within the bound.
A program may use at most 64 MiB of HBM per device.

```python
import math
import jax
import jax.numpy as jnp
import numpy as np
from jax import lax

R_OUT = 64
R_IN = 64
MODULES = 16
F = 65536
QUERIES = 1024
TR_DEV = 1024
TRAIN = 8192
N_EX = 8


def factor_table(key, order, top):
    first, second = jax.random.split(key)
    diagonal = jnp.exp(jax.random.uniform(first, (MODULES, order), jnp.float32, 0.0, jnp.log(top)))
    noise = jax.random.truncated_normal(second, -3.0, 3.0, (MODULES, order, order), jnp.float32) * (0.35 / order ** 0.5)
    unit = (jnp.arange(order)[:, None] == jnp.arange(order)[None, :]).astype(jnp.float32)
    return noise * (1.0 - unit) + unit * diagonal[:, :, None]


def draw_inv_out(key, part):
    key = jax.random.fold_in(key, 11)
    return factor_table(key, R_OUT, 2.0)


def draw_inv_in(key, part):
    key = jax.random.fold_in(key, 23)
    return factor_table(key, R_IN, 2.0)


def raised(result, key, source, target, shards_of, factor):
    def block_of(dim):
        return (jnp.arange(result.shape[dim]) // (result.shape[dim] // shards_of)).reshape((-1,) + (1,) * (result.ndim - 1 - dim))

    near = jax.random.permutation(key, shards_of)[block_of(target)]
    other_side = (block_of(target) + shards_of // 2) % shards_of
    return jnp.where((block_of(source) == near) | (block_of(source) == other_side), factor * result, result)


def block_levels(own_key, shape, cuts, least, largest):
    def one(position, parts):
        heights = jax.random.uniform(jax.random.fold_in(jax.random.fold_in(own_key, 6), position), (parts,), jnp.float32, least / len(cuts), largest / len(cuts))
        return jnp.repeat(jnp.exp(heights), shape[position] // parts).reshape((-1,) + (1,) * (len(shape) - position - 1))

    gain = one(*cuts[0])
    for cut in cuts[1:]:
        gain = gain * one(*cut)
    return gain


def split_up(count, total, bound, slope):
    weights = [(1 << 20) // math.isqrt(grade ** slope) + 1 for grade in range(2, count + 1)]
    rest, holding = total - bound - (count - 1), [1] * (count - 1)
    while rest > 0:
        candidates = [i for i in range(count - 1) if holding[i] < bound]
        whole, remaining = sum([weights[i] for i in candidates]), rest
        for i in candidates:
            extra = min(bound - holding[i], max(1, remaining * weights[i] // whole), rest)
            holding[i] = holding[i] + extra
            rest = rest - extra
    return np.array([bound] + holding)


def ragged_sizes(stream_key, number_of, total, most, skew):
    if number_of == 2:
        one = jax.random.randint(stream_key, (), max(1, total - most), min(most, total - 1) + 1)
        return jnp.stack([one, total - one])
    sizes = jnp.asarray(split_up(number_of, total, most, skew), jnp.int32)
    couples = (number_of - 1) // 2
    source_of, taker = sizes[1:1 + 2 * couples:2], sizes[2:2 + 2 * couples:2]
    margin = jnp.minimum(source_of - 1, most - taker)
    shifted = jax.random.randint(jax.random.fold_in(stream_key, 1), (couples,), 0, 1 << 20) % (margin + 1)
    sizes = sizes.at[1:1 + 2 * couples:2].set(source_of - shifted).at[2:2 + 2 * couples:2].set(taker + shifted)
    return sizes[jax.random.permutation(jax.random.fold_in(stream_key, 2), number_of)]


def centred(stream_key, extent, spread, reach, cuts=(), kind=jnp.bfloat16):
    array = jax.random.normal(stream_key, extent, jnp.float32) * spread
    if len(cuts) > 0:
        array = block_levels(stream_key, extent, cuts, -0.22, 0.18) * array
    return jnp.clip(array, min=-reach, max=reach).astype(kind)


def heavy_noise(own_key, dims, spread, reach, cuts, heavy, kind=jnp.bfloat16):
    result = spread * jax.random.normal(own_key, dims, jnp.float32)
    if cuts:
        result = result * block_levels(own_key, dims, cuts, -0.22, 0.18)
    return jnp.clip(raised(result, jax.random.fold_in(own_key, 3), *heavy), -reach, reach).astype(kind)


def setup_inputs(seed: int = 0) -> dict:
    splits = jax.random.split(jax.random.key(seed), 6)
    return {
        "train_grads": centred(splits[0], (TRAIN, F), 1.0, 6.0, ((0, 8), (1, 32))),
        "queries": heavy_noise(splits[1], (QUERIES, F), 1.0, 24.0, ((0, 256),), (1, 0, 256, 6.0)),
        "inv_out": draw_inv_out(jax.random.fold_in(splits[5], 71), 0),
        "inv_in": draw_inv_in(jax.random.fold_in(splits[5], 71), 0),
        "module_rank": ragged_sizes(splits[4], MODULES, MODULES * R_OUT * 3 // 4, R_OUT, 0).astype(jnp.int32),
    }


def precondition(queries, inv_out, inv_in, module_rank):
    count = queries.shape[0]
    modules, rows, _ = inv_out.shape
    cols = inv_in.shape[1]
    as_float = queries.astype(jnp.float32).reshape(count, modules, rows, cols)
    left = jnp.einsum("mab,qmbc->qmac", inv_out, as_float, precision=lax.Precision.HIGHEST)
    mixed = jnp.einsum("qmac,mcd->qmad", left, inv_in, precision=lax.Precision.HIGHEST)
    live = (jnp.arange(rows, dtype=jnp.int32)[None, :] < module_rank[:, None]).astype(jnp.float32)
    masked = mixed * live[None, :, :, None]
    return masked.astype(jnp.bfloat16).reshape(count, modules * rows * cols)


def reference(train_grads, queries, inv_out, inv_in, module_rank):
    conditioned = precondition(queries, inv_out, inv_in, module_rank)
    scale = float(F) ** -0.5

    def score_block(rows):
        return jnp.dot(rows, conditioned.T, preferred_element_type=jnp.float32) * scale

    blocks = lax.map(score_block, train_grads.reshape(N_EX, TR_DEV, F))
    return blocks.reshape(TRAIN, QUERIES)
```

```python
import jax
import jax.numpy as jnp
from jax import lax
from jax.experimental import pallas as pl
from jax.experimental.pallas import tpu as pltpu
from jax.sharding import PartitionSpec as P

MESH = pl.DeviceIdType.MESH
F32 = jnp.float32
BF16 = jnp.bfloat16
ORDER = (0, 1, 3, 2)


def dot(a, b):
    return jnp.dot(a, b, preferred_element_type=F32)


def dot_t(a, b):
    return lax.dot_general(a, b, (((1,), (1,)), ((), ())), preferred_element_type=F32)


def halves(value):
    high = value.astype(BF16)
    return high, (value - high.astype(F32)).astype(BF16)


def where_ones(mask):
    return jnp.where(mask, 1.0, 0.0).astype(BF16)


def kernel(
    train, queries, inv_out, inv_in, ranks, out,
    train_v, raw, factor, spread, mixed_in, mixed_out, cond, other, part, pair, out_y, in_y, out_z, in_z,
    local_sem, raw_send, raw_recv, mate_send, mate_recv, zlo_send, zlo_recv, x_send, x_recv,
    pair_send, pair_recv, y_send, y_recv, z_send, z_recv,
):
    ex, feat = lax.axis_index("ex"), lax.axis_index("feat")
    core = feat % 2
    module = feat // 2
    y = module % 4
    z_hi = module // 4
    z_lo = ex % 2
    mate = feat + 1 - 2 * core
    ex_z = ex + 1 - 2 * z_lo
    ex_up, ex_down, ex_far = (ex + 2) % 8, (ex + 6) % 8, (ex + 4) % 8

    def remote(src, dst, send, recv, to_ex, to_feat):
        return pltpu.make_async_remote_copy(
            src_ref=src, dst_ref=dst, send_sem=send, recv_sem=recv, device_id=(to_ex, to_feat), device_id_type=MESH
        )

    def arrived(ref, sem):
        pltpu.make_async_copy(ref, ref, sem).wait()

    own_raw = pltpu.make_async_copy(
        queries.at[:, pl.ds(pl.multiple_of(module * 4096, 4096), 4096)], raw.at[0, y], raw_recv.at[0, y]
    )
    own_raw.start()
    load_out = pltpu.make_async_copy(inv_out.at[module], factor.at[0], local_sem.at[0])
    load_in = pltpu.make_async_copy(inv_in.at[module], factor.at[1], local_sem.at[1])
    load_train = pltpu.make_async_copy(train, train_v, local_sem.at[2])
    load_out.start()
    load_in.start()
    load_train.start()

    barrier = pltpu.get_barrier_semaphore()

    def greet(i, carry):
        pl.semaphore_signal(barrier, inc=1, device_id=(ex, (feat + i) % 32), device_id_type=MESH)
        return carry

    lax.fori_loop(1, 32, greet, 0)
    for peer in (ex_z, ex_up, ex_down):
        pl.semaphore_signal(barrier, inc=1, device_id=(peer, feat), device_id_type=MESH)
    pl.semaphore_wait(barrier, 34)

    sends = []

    def send(*args):
        copy = remote(*args)
        copy.start()
        sends.append(copy)

    for dz in ORDER:
        for dy in range(4):
            if dz == 0 and dy == 0:
                continue
            to_module = (z_hi + 4 - dz) % 4 * 4 + (y + dy) % 4
            send(
                queries.at[:, pl.ds(pl.multiple_of(to_module * 4096, 4096), 4096)],
                raw.at[dz, y], raw_send.at[dz, dy], raw_recv.at[dz, y], ex, to_module * 2 + core,
            )

    load_out.wait()
    load_in.wait()
    r_row = lax.broadcasted_iota(jnp.int32, (64, 64), 0)
    r_col = lax.broadcasted_iota(jnp.int32, (64, 64), 1)
    place = where_ones(r_row == jnp.where(r_col < 32, 2 * r_col, 2 * r_col - 63))
    place_t = where_ones(r_col == jnp.where(r_row < 32, 2 * r_row, 2 * r_row - 63))
    left = []
    for term in halves(factor[0]):
        turned = dot(term, place).astype(BF16)
        left.append(dot(place_t, turned).astype(BF16))
    tall = where_ones(
        lax.broadcasted_iota(jnp.int32, (256, 64), 0) % 64 == lax.broadcasted_iota(jnp.int32, (256, 64), 1)
    )
    wide = where_ones(
        lax.broadcasted_iota(jnp.int32, (64, 256), 1) % 64 == lax.broadcasted_iota(jnp.int32, (64, 256), 0)
    )
    same = (
        lax.broadcasted_iota(jnp.int32, (256, 256), 0) // 64 == lax.broadcasted_iota(jnp.int32, (256, 256), 1) // 64
    )
    right = []
    for term in halves(factor[1]):
        full = dot(dot(tall, term).astype(BF16), wide)
        right.append(jnp.where(same, full, 0.0).astype(BF16))
    rows = lax.broadcasted_iota(jnp.int32, (256, 256), 0) % 64
    row = jnp.where(rows < 32, 2 * rows, 2 * rows - 63)
    live = jnp.where(row < ranks[module], 1.0, 0.0).astype(F32)
    low = lax.broadcasted_iota(jnp.int32, (32, 128), 1) < 64

    def own_rows(e, start, count):
        return pl.ds(pl.multiple_of(e * 32 + start, 16), count)

    def precondition(k):
        for ys in range(4):
            arrived(raw.at[k, ys], raw_recv.at[k, ys])
        for ys in range(4):
            block = raw[k, ys].astype(F32)
            for r in range(32):
                spread[ys * 128 + 4 * r : ys * 128 + 4 * r + 4, :] = block[:, r * 128 : (r + 1) * 128]
        for p in range(8):
            first = (p // 2) * 128 + 2 * (p % 2)
            a = spread[pl.ds(first, 32, stride=4), :]
            b = spread[pl.ds(first + 1, 32, stride=4), :]
            lanes = slice(p * 128, (p + 1) * 128)
            mixed_in[0:32, lanes] = jnp.where(low, a, pltpu.roll(b, 64, 1)).astype(BF16)
            mixed_in[32:64, lanes] = jnp.where(low, pltpu.roll(a, 64, 1), b).astype(BF16)
        value = mixed_in[...]
        turned = dot(left[0], value) + dot(left[1], value)
        high, rest = halves(jnp.concatenate([turned[:, g * 256 : (g + 1) * 256] for g in range(4)], axis=0))
        mixed = (dot(high, right[0]) + (dot(rest, right[0]) + dot(high, right[1]))) * live
        for p in range(8):
            g, lanes = p // 2, slice(p % 2 * 128, (p % 2 + 1) * 128)
            even = mixed[g * 64 : g * 64 + 32, lanes]
            odd = mixed[g * 64 + 32 : g * 64 + 64, lanes]
            mixed_out[64 * p : 64 * p + 32, :] = jnp.where(low, even, pltpu.roll(odd, 64, 1))
            mixed_out[64 * p + 32 : 64 * p + 64, :] = jnp.where(low, pltpu.roll(even, 64, 1), odd)
        for i in range(16):
            lanes = slice(i * 128, (i + 1) * 128)
            other[k, :, lanes] = mixed_out[pl.ds((1 - core) * 16 + i, 16, stride=32), :].astype(BF16)
        mine = own_rows(ex, core * 16, 16)
        send(other.at[k], cond.at[k, mine], mate_send.at[k], mate_recv.at[k], ex, mate)
        for i in range(16):
            lanes = slice(i * 128, (i + 1) * 128)
            cond[k, mine, lanes] = mixed_out[pl.ds(core * 16 + i, 16, stride=32), :].astype(BF16)

    def to_x(k, rows_, way, what):
        ref = cond.at[k, rows_]
        send(ref, ref, x_send.at[k, way, what], x_recv.at[k, way, what], (ex_up, ex_down)[way], feat)

    def from_x(k, rows_, way, what):
        arrived(cond.at[k, rows_], x_recv.at[k, way, what])

    def first_hop(k):
        arrived(cond.at[k, own_rows(ex, (1 - core) * 16, 16)], mate_recv.at[k])
        ref = cond.at[k, own_rows(ex, 0, 32)]
        send(ref, ref, zlo_send.at[k], zlo_recv.at[k], ex_z, feat)
        to_x(k, own_rows(ex, 0, 32), 0, 0)
        to_x(k, own_rows(ex, 0, 32), 1, 0)

    def second_hop(k):
        arrived(cond.at[k, own_rows(ex_z, 0, 32)], zlo_recv.at[k])
        to_x(k, own_rows(ex_z, 0, 32), 0, 1)
        to_x(k, own_rows(ex_z, 0, 32), 1, 1)

    def swap(e):
        return e + 1 - 2 * z_lo

    def forward(k, what):
        below = ex_down if what == 0 else swap(ex_down)
        above = ex_up if what == 0 else swap(ex_up)
        from_x(k, own_rows(below, 0, 32), 0, what)
        to_x(k, own_rows(below, 0, 16), 0, what + 2)
        from_x(k, own_rows(above, 0, 32), 1, what)
        to_x(k, own_rows(above, 16, 16), 1, what + 2)

    def multiply(k):
        for what in range(2):
            far = ex_far if what == 0 else swap(ex_far)
            from_x(k, own_rows(far, 0, 16), 0, what + 2)
            from_x(k, own_rows(far, 16, 16), 1, what + 2)

        def tile(t, carry):
            at = pl.ds(pl.multiple_of(t * 256, 256), 256)
            part[k, :, at] = dot_t(cond[k], train_v[at, :])
            return carry

        lax.fori_loop(0, 4, tile, 0)
        give = pl.ds(pl.multiple_of((1 - core) * 128, 128), 128)
        send(part.at[k, give], pair.at[k], pair_send.at[k], pair_recv.at[k], ex, mate)

    def block_of(y_):
        return 2 * (y_ % 2) + y_ // 2

    def summed(k, y_):
        at = pl.multiple_of(block_of(y_) * 32, 32)
        return part[k, pl.ds(pl.multiple_of(core * 128 + at, 32), 32), :] + pair[k, pl.ds(at, 32), :]

    def reduce_y(k):
        arrived(pair.at[k], pair_recv.at[k])
        for dy in range(1, 4):
            to_y = (y + dy) % 4
            out_y[k, dy - 1] = summed(k, to_y).astype(BF16)
            send(
                out_y.at[k, dy - 1], in_y.at[k, dy - 1], y_send.at[k, dy - 1], y_recv.at[k, dy - 1],
                ex, (z_hi * 4 + to_y) * 2 + core,
            )

    late = []

    def reduce_z(k):
        total = summed(k, y)
        for dy in range(1, 4):
            arrived(in_y.at[k, dy - 1], y_recv.at[k, dy - 1])
            total = total + in_y[k, dy - 1].astype(F32)
        owner = 4 * (4 * core + block_of(y)) + (z_hi + k) % 4
        out_z[k] = total.astype(BF16)
        copy = remote(out_z.at[k], in_z.at[z_hi], z_send.at[k], z_recv.at[z_hi], ex, owner)
        late.append((owner, copy))

        @pl.when(owner != feat)
        def _():
            copy.start()

        @pl.when(owner == feat)
        def _():
            in_z[z_hi] = out_z[k]

    a, b, c, d = ORDER
    precondition(a)
    first_hop(a)
    precondition(b)
    first_hop(b)
    second_hop(a)
    forward(a, 0)
    precondition(c)
    first_hop(c)
    second_hop(b)
    forward(a, 1)
    forward(b, 0)
    precondition(d)
    first_hop(d)
    second_hop(c)
    forward(b, 1)
    load_train.wait()
    multiply(a)
    forward(c, 0)
    second_hop(d)
    reduce_y(a)
    forward(c, 1)
    multiply(b)
    forward(d, 0)
    reduce_z(a)
    reduce_y(b)
    forward(d, 1)
    multiply(c)
    reduce_z(b)
    reduce_y(c)
    multiply(d)
    reduce_z(c)
    reduce_y(d)
    reduce_z(d)

    mine = feat // 4
    total = None
    for zs in range(4):
        sender = (zs * 4 + 2 * (mine % 2) + mine // 2 % 2) * 2 + mine // 4

        @pl.when(sender != feat)
        def _():
            arrived(in_z.at[zs], z_recv.at[zs])

        value = in_z[zs].astype(F32)
        total = value if total is None else total + value
    total = total * (65536.0 ** -0.5)
    for cs in range(2):
        for ys in range(4):
            at = (ys * 2 + cs) * 4
            out[at : at + 4, :] = total[cs * 16 + ys * 4 : cs * 16 + ys * 4 + 4, :]

    for copy in sends:
        copy.wait_send()
    for owner, copy in late:

        @pl.when(owner != feat)
        def _():
            copy.wait_send()


def on_device(train_grads, queries, inv_out, inv_in, module_rank):
    any_space = pl.BlockSpec(memory_space=pl.ANY)
    dma = pltpu.SemaphoreType.DMA
    result = pl.pallas_call(
        kernel,
        out_shape=jax.ShapeDtypeStruct((32, 1024), F32),
        in_specs=[any_space] * 4 + [pl.BlockSpec(memory_space=pltpu.SMEM)],
        out_specs=pl.BlockSpec(memory_space=pltpu.VMEM),
        scratch_shapes=[
            pltpu.VMEM((1024, 2048), BF16),
            pltpu.VMEM((4, 4, 4, 4096), BF16),
            pltpu.VMEM((2, 64, 64), F32),
            pltpu.VMEM((512, 128), F32),
            pltpu.VMEM((64, 1024), BF16),
            pltpu.VMEM((512, 128), F32),
            pltpu.VMEM((4, 256, 2048), BF16),
            pltpu.VMEM((4, 16, 2048), BF16),
            pltpu.VMEM((4, 256, 1024), F32),
            pltpu.VMEM((4, 128, 1024), F32),
            pltpu.VMEM((4, 3, 32, 1024), BF16),
            pltpu.VMEM((4, 3, 32, 1024), BF16),
            pltpu.VMEM((4, 32, 1024), BF16),
            pltpu.VMEM((4, 32, 1024), BF16),
            dma((3,)),
            dma((4, 4)), dma((4, 4)),
            dma((4,)), dma((4,)),
            dma((4,)), dma((4,)),
            dma((4, 2, 4)), dma((4, 2, 4)),
            dma((4,)), dma((4,)),
            dma((4, 3)), dma((4, 3)),
            dma((4,)), dma((4,)),
        ],
        compiler_params=pltpu.CompilerParams(
            collective_id=0, has_side_effects=True, vmem_limit_bytes=48 * 1024 * 1024
        ),
        cost_estimate=pl.CostEstimate(flops=2 * 1024 * 1024 * 2048, bytes_accessed=8 * 1024 * 1024, transcendentals=0),
    )(train_grads, queries, inv_out, inv_in, module_rank)
    return result.T


def solution(mesh):
    return jax.shard_map(
        on_device,
        mesh=mesh,
        in_specs=(P("ex", "feat"), P(("ex", "feat"), None), P(), P(), P()),
        out_specs=P("ex", "feat"),
        check_vma=False,
    )
```

```python
import jax
import jax.numpy as jnp
from jax import lax
from jax.experimental import pallas as pl
from jax.experimental.pallas import tpu as pltpu
from jax.sharding import PartitionSpec as P

MESH = pl.DeviceIdType.MESH
F32 = jnp.float32
BF16 = jnp.bfloat16
TS = 1
TW = 1024 // TS
XZ = (0,)


def dot(a, b):
    return jnp.dot(a, b, preferred_element_type=F32)


def dot_t(a, b):
    return lax.dot_general(a, b, (((1,), (1,)), ((), ())), preferred_element_type=F32)


def halves(value):
    high = value.astype(BF16)
    return high, (value - high.astype(F32)).astype(BF16)


def where_ones(mask):
    return jnp.where(mask, 1.0, 0.0).astype(BF16)


def kernel(
    train, queries, inv_out, inv_in, ranks, out,
    train_v, raw, factor, spread, mixed_in, mixed_out, cond, other, part, pair, out_y, in_y, out_z, in_z,
    local_sem, raw_send, raw_recv, mate_send, mate_recv, zlo_send, zlo_recv, x_send, x_recv,
    pair_send, pair_recv, y_send, y_recv, z_send, z_recv,
):
    ex, feat = lax.axis_index("ex"), lax.axis_index("feat")
    core = lax.rem(feat, 2)
    module = feat // 2
    y = lax.rem(module, 4)
    z_hi = module // 4
    z_lo = lax.rem(ex, 2)
    mate = feat + 1 - 2 * core
    ex_z = ex + 1 - 2 * z_lo
    ex_up, ex_down, ex_far = lax.rem(ex + 2, 8), lax.rem(ex + 6, 8), lax.rem(ex + 4, 8)

    def remote(src, dst, send, recv, to_ex, to_feat):
        return pltpu.make_async_remote_copy(
            src_ref=src, dst_ref=dst, send_sem=send, recv_sem=recv, device_id=(to_ex, to_feat), device_id_type=MESH
        )

    def arrived(ref, sem):
        pltpu.make_async_copy(ref, ref, sem).wait()

    own_raw = pltpu.make_async_copy(
        queries.at[:, pl.ds(pl.multiple_of(module * 4096, 4096), 4096)], raw.at[0, y], raw_recv.at[0, y]
    )
    own_raw.start()
    load_out = pltpu.make_async_copy(inv_out.at[module], factor.at[0], local_sem.at[0])
    load_in = pltpu.make_async_copy(inv_in.at[module], factor.at[1], local_sem.at[1])
    load_train = pltpu.make_async_copy(train, train_v, local_sem.at[2])
    load_out.start()
    load_in.start()

    barrier = pltpu.get_barrier_semaphore()

    for dz in range(4):
        for dy in range(4):
            if (dz, dy) != (0, 0):
                peer = (lax.rem(z_hi + dz, 4) * 4 + lax.rem(y + dy, 4)) * 2 + core
                pl.semaphore_signal(barrier, inc=1, device_id=(ex, peer), device_id_type=MESH)
    pl.semaphore_signal(barrier, inc=1, device_id=(ex, mate), device_id_type=MESH)
    for peer in (ex_z, ex_up, ex_down):
        pl.semaphore_signal(barrier, inc=1, device_id=(peer, feat), device_id_type=MESH)
    pl.semaphore_wait(barrier, 19)

    sends = []

    def send(*args):
        copy = remote(*args)
        copy.start()
        sends.append(copy)

    def send_raw(dz, dy):
        to_module = lax.rem(z_hi + 4 - dz, 4) * 4 + lax.rem(y + dy, 4)
        send(
            queries.at[:, pl.ds(pl.multiple_of(to_module * 4096, 4096), 4096)],
            raw.at[dz, y], raw_send.at[dz, dy], raw_recv.at[dz, y], ex, to_module * 2 + core,
        )

    def raw_out(dz):
        for dy in (2, 1, 3, 0):
            if (dz, dy) != (0, 0):
                send_raw(dz, dy)

    for first in (0, 1, 3,):
        raw_out(first)

    load_train.start()
    load_out.wait()
    load_in.wait()
    r_row = lax.broadcasted_iota(jnp.int32, (64, 64), 0)
    r_col = lax.broadcasted_iota(jnp.int32, (64, 64), 1)
    place = where_ones(r_row == jnp.where(r_col < 32, 2 * r_col, 2 * r_col - 63))
    place_t = where_ones(r_col == jnp.where(r_row < 32, 2 * r_row, 2 * r_row - 63))
    left = []
    for term in halves(factor[0]):
        turned = dot(term, place).astype(BF16)
        left.append(dot(place_t, turned).astype(BF16))
    tall = where_ones(
        lax.broadcasted_iota(jnp.int32, (256, 64), 0) % 64 == lax.broadcasted_iota(jnp.int32, (256, 64), 1)
    )
    wide = where_ones(
        lax.broadcasted_iota(jnp.int32, (64, 256), 1) % 64 == lax.broadcasted_iota(jnp.int32, (64, 256), 0)
    )
    same = (
        lax.broadcasted_iota(jnp.int32, (256, 256), 0) // 64 == lax.broadcasted_iota(jnp.int32, (256, 256), 1) // 64
    )
    right = []
    for term in halves(factor[1]):
        full = dot(dot(tall, term).astype(BF16), wide)
        right.append(jnp.where(same, full, 0.0).astype(BF16))
    rows = lax.broadcasted_iota(jnp.int32, (256, 256), 0) % 64
    row = jnp.where(rows < 32, 2 * rows, 2 * rows - 63)
    live = jnp.where(row < ranks[module], 1.0, 0.0).astype(F32)
    low = lax.broadcasted_iota(jnp.int32, (32, 128), 1) < 64

    def own_rows(e, start, count):
        return pl.ds(pl.multiple_of(lax.rem(e + 8 - 2 * z_hi, 8) * 32 + start, 16), count)

    def precondition(k):
        for ys in range(4):
            arrived(raw.at[k, ys], raw_recv.at[k, ys])
        for ys in range(4):
            block = raw[k, ys].astype(F32)
            for r in range(32):
                spread[ys * 128 + 4 * r : ys * 128 + 4 * r + 4, :] = block[:, r * 128 : (r + 1) * 128]
        for p in range(8):
            first = (p // 2) * 128 + 2 * (p % 2)
            a = spread[pl.ds(first, 32, stride=4), :]
            b = spread[pl.ds(first + 1, 32, stride=4), :]
            lanes = slice(p * 128, (p + 1) * 128)
            mixed_in[0:32, lanes] = jnp.where(low, a, pltpu.roll(b, 64, 1)).astype(BF16)
            mixed_in[32:64, lanes] = jnp.where(low, pltpu.roll(a, 64, 1), b).astype(BF16)
        value = mixed_in[...]
        turned = dot(left[0], value) + dot(left[1], value)
        high, rest = halves(jnp.concatenate([turned[:, g * 256 : (g + 1) * 256] for g in range(4)], axis=0))
        mixed = (dot(high, right[0]) + (dot(rest, right[0]) + dot(high, right[1]))) * live
        for p in range(8):
            g, lanes = p // 2, slice(p % 2 * 128, (p % 2 + 1) * 128)
            even = mixed[g * 64 : g * 64 + 32, lanes]
            odd = mixed[g * 64 + 32 : g * 64 + 64, lanes]
            mixed_out[64 * p : 64 * p + 32, :] = jnp.where(low, even, pltpu.roll(odd, 64, 1))
            mixed_out[64 * p + 32 : 64 * p + 64, :] = jnp.where(low, pltpu.roll(even, 64, 1), odd)
        for i in range(16):
            lanes = slice(i * 128, (i + 1) * 128)
            other[k, :, lanes] = mixed_out[pl.ds((1 - core) * 16 + i, 16, stride=32), :].astype(BF16)
        mine = own_rows(ex, core * 16, 16)
        send(other.at[k], cond.at[k, mine], mate_send.at[k], mate_recv.at[k], ex, mate)
        for i in range(16):
            lanes = slice(i * 128, (i + 1) * 128)
            cond[k, mine, lanes] = mixed_out[pl.ds(core * 16 + i, 16, stride=32), :].astype(BF16)

    def to_x(k, rows_, way, what):
        ref = cond.at[k, rows_]
        send(ref, ref, x_send.at[k, way, what], x_recv.at[k, way, what], (ex_up, ex_down)[way], feat)

    def from_x(k, rows_, way, what):
        arrived(cond.at[k, rows_], x_recv.at[k, way, what])

    def to_z(k, rows_, what):
        ref = cond.at[k, rows_]
        send(ref, ref, zlo_send.at[k, what], zlo_recv.at[k, what], ex_z, feat)

    def from_z(k, rows_, what):
        arrived(cond.at[k, rows_], zlo_recv.at[k, what])

    def first_hop(k):
        to_x(k, own_rows(ex, 0, 32), 0, 0)
        to_x(k, own_rows(ex, 0, 32), 1, 0)

    def side(k):
        to_z(k, own_rows(ex, 0, 32), 0)

    def second_hop(k):
        from_z(k, own_rows(ex_z, 0, 32), 0)
        to_x(k, own_rows(ex_z, 0, 32), 0, 1)
        to_x(k, own_rows(ex_z, 0, 32), 1, 1)

    def swap(e):
        return e + 1 - 2 * z_lo

    def forward(k, what):
        below = ex_down if what == 0 else swap(ex_down)
        above = ex_up if what == 0 else swap(ex_up)
        from_x(k, own_rows(below, 0, 32), 0, what)
        to_x(k, own_rows(below, 0, 16), 0, what + 2)
        from_x(k, own_rows(above, 0, 32), 1, what)
        to_x(k, own_rows(above, 16, 16), 1, what + 2)

    def near_to_z(k):
        to_z(k, own_rows(ex_down, 0, 32), 1)
        to_z(k, own_rows(ex_up, 0, 32), 2)

    def far_to_z(k):
        from_x(k, own_rows(ex_far, 0, 16), 0, 2)
        to_z(k, own_rows(ex_far, 0, 16), 3)
        from_x(k, own_rows(ex_far, 16, 16), 1, 2)
        to_z(k, own_rows(ex_far, 16, 16), 4)

    def complete(k):
        if k in XZ:
            from_z(k, own_rows(ex_z, 0, 32), 0)
            from_z(k, own_rows(swap(ex_down), 0, 32), 1)
            from_z(k, own_rows(swap(ex_up), 0, 32), 2)
            from_z(k, own_rows(swap(ex_far), 0, 16), 3)
            from_z(k, own_rows(swap(ex_far), 16, 16), 4)
        else:
            for what in range(2):
                far = ex_far if what == 0 else swap(ex_far)
                from_x(k, own_rows(far, 0, 16), 0, what + 2)
                from_x(k, own_rows(far, 16, 16), 1, what + 2)

    def multiply(k, t):
        part[k, t] = dot_t(cond[k], train_v[t * TW : (t + 1) * TW, :])
        give = pl.ds(pl.multiple_of((1 - core) * 128, 128), 128)
        send(part.at[k, t, give], pair.at[k, t], pair_send.at[k, t], pair_recv.at[k, t], ex, mate)

    def block_of(y_):
        return 2 * (y_ % 2) + y_ // 2

    def summed(k, t, y_):
        at = pl.multiple_of(block_of(y_) * 32, 32)
        return part[k, t, pl.ds(pl.multiple_of(core * 128 + at, 32), 32), :] + pair[k, t, pl.ds(at, 32), :]

    def reduce_y(k, t):
        arrived(pair.at[k, t], pair_recv.at[k, t])
        for dy in (2, 1, 3):
            to_y = lax.rem(y + dy, 4)
            out_y[k, t, dy - 1] = summed(k, t, to_y).astype(BF16)
            send(
                out_y.at[k, t, dy - 1], in_y.at[k, t, dy - 1], y_send.at[k, t, dy - 1], y_recv.at[k, t, dy - 1],
                ex, (z_hi * 4 + to_y) * 2 + core,
            )

    late = []

    def reduce_z(k, t):
        total = summed(k, t, y)
        for dy in (1, 3, 2):
            arrived(in_y.at[k, t, dy - 1], y_recv.at[k, t, dy - 1])
            total = total + in_y[k, t, dy - 1].astype(F32)
        owner = 4 * lax.rem(4 * core + block_of(y) + 2 * z_hi, 8) + lax.rem(z_hi + k, 4)
        out_z[k, t] = total.astype(BF16)
        copy = remote(out_z.at[k, t], in_z.at[z_hi, t], z_send.at[k, t], z_recv.at[z_hi, t], ex, owner)
        late.append((owner, copy))

        @pl.when(owner != feat)
        def _():
            copy.start()

        @pl.when(owner == feat)
        def _():
            in_z[z_hi, t] = out_z[k, t]

    def from_mate(k):
        arrived(cond.at[k, own_rows(ex, (1 - core) * 16, 16)], mate_recv.at[k])

    precondition(0)
    from_mate(0)
    first_hop(0)
    raw_out(2)
    forward(0, 0)
    precondition(1)
    from_mate(1)
    first_hop(1)
    side(1)
    precondition(3)
    from_mate(3)
    side(3)
    forward(1, 0)
    second_hop(1)
    first_hop(3)
    precondition(2)
    from_mate(2)
    side(2)
    forward(1, 1)
    forward(3, 0)
    second_hop(3)
    first_hop(2)
    load_train.wait()
    complete(1)
    multiply(1, 0)
    side(0)
    near_to_z(0)
    far_to_z(0)
    forward(3, 1)
    forward(2, 0)
    second_hop(2)
    reduce_y(1, 0)
    complete(3)
    multiply(3, 0)
    reduce_z(1, 0)
    forward(2, 1)
    reduce_y(3, 0)
    complete(0)
    multiply(0, 0)
    reduce_z(3, 0)
    reduce_y(0, 0)
    complete(2)
    multiply(2, 0)
    reduce_y(2, 0)
    reduce_z(0, 0)
    reduce_z(2, 0)

    mine = feat // 4
    for t in range(TS):
        total = None
        for zs in range(4):
            place_ = lax.rem(mine + 8 - 2 * zs, 8)
            sender = (zs * 4 + 2 * lax.rem(place_, 2) + lax.rem(place_ // 2, 2)) * 2 + place_ // 4

            @pl.when(sender != feat)
            def _():
                arrived(in_z.at[zs, t], z_recv.at[zs, t])

            value = in_z[zs, t].astype(F32)
            total = value if total is None else total + value
        total = total * (65536.0 ** -0.5)
        for cs in range(2):
            for ys in range(4):
                at = (ys * 2 + cs) * 4
                out[at : at + 4, t * TW : (t + 1) * TW] = total[cs * 16 + ys * 4 : cs * 16 + ys * 4 + 4, :]

    for copy in sends:
        copy.wait_send()
    for owner, copy in late:

        @pl.when(owner != feat)
        def _():
            copy.wait_send()


def on_device(train_grads, queries, inv_out, inv_in, module_rank):
    any_space = pl.BlockSpec(memory_space=pltpu.HBM)
    dma = pltpu.SemaphoreType.DMA
    result = pl.pallas_call(
        kernel,
        out_shape=jax.ShapeDtypeStruct((32, 1024), F32),
        in_specs=[any_space] * 4 + [pl.BlockSpec(memory_space=pltpu.SMEM)],
        out_specs=pl.BlockSpec(memory_space=pltpu.VMEM),
        scratch_shapes=[
            pltpu.VMEM((1024, 2048), BF16),
            pltpu.VMEM((4, 4, 4, 4096), BF16),
            pltpu.VMEM((2, 64, 64), F32),
            pltpu.VMEM((512, 128), F32),
            pltpu.VMEM((64, 1024), BF16),
            pltpu.VMEM((512, 128), F32),
            pltpu.VMEM((4, 256, 2048), BF16),
            pltpu.VMEM((4, 16, 2048), BF16),
            pltpu.VMEM((4, TS, 256, TW), F32),
            pltpu.VMEM((4, TS, 128, TW), F32),
            pltpu.VMEM((4, TS, 3, 32, TW), BF16),
            pltpu.VMEM((4, TS, 3, 32, TW), BF16),
            pltpu.VMEM((4, TS, 32, TW), BF16),
            pltpu.VMEM((4, TS, 32, TW), BF16),
            dma((3,)),
            dma((4, 4)), dma((4, 4)),
            dma((4,)), dma((4,)),
            dma((4, 5)), dma((4, 5)),
            dma((4, 2, 4)), dma((4, 2, 4)),
            dma((4, TS)), dma((4, TS)),
            dma((4, TS, 3)), dma((4, TS, 3)),
            dma((4, TS)), dma((4, TS)),
        ],
        compiler_params=pltpu.CompilerParams(
            collective_id=0, has_side_effects=True, vmem_limit_bytes=60 * 1024 * 1024
        ),
        cost_estimate=pl.CostEstimate(flops=2 * 1024 * 1024 * 2048, bytes_accessed=8 * 1024 * 1024, transcendentals=0),
    )(train_grads, queries, inv_out, inv_in, module_rank)
    return result.T


def solution(mesh):
    return jax.shard_map(
        on_device,
        mesh=mesh,
        in_specs=(P("ex", "feat"), P(("ex", "feat"), None), P(), P(), P()),
        out_specs=P("ex", "feat"),
        check_vma=False,
    )
```

```python
import jax
import jax.numpy as jnp
from jax import lax
from jax.experimental import pallas as pl
from jax.experimental.pallas import tpu as pltpu
from jax.sharding import PartitionSpec as P

MESH = pl.DeviceIdType.MESH
F32 = jnp.float32
BF16 = jnp.bfloat16
TS = 1
TW = 1024 // TS
XZ = (0,)
DIRECT = (2,)


def dot(a, b):
    return jnp.dot(a, b, preferred_element_type=F32)


def dot_t(a, b):
    return lax.dot_general(a, b, (((1,), (1,)), ((), ())), preferred_element_type=F32)


def halves(value):
    high = value.astype(BF16)
    return high, (value - high.astype(F32)).astype(BF16)


def where_ones(mask):
    return jnp.where(mask, 1.0, 0.0).astype(BF16)


def kernel(
    train, queries, inv_out, inv_in, ranks, out,
    train_v, raw, factor, spread, mixed_in, mixed_out, cond, other, part, pair, out_y, in_y, out_z, in_z,
    local_sem, raw_send, raw_recv, mate_send, mate_recv, zlo_send, zlo_recv, x_send, x_recv, first_send, first_recv,
    pair_send, pair_recv, y_send, y_recv, z_send, z_recv,
):
    ex, feat = lax.axis_index("ex"), lax.axis_index("feat")
    core = lax.rem(feat, 2)
    module = feat // 2
    y = lax.rem(module, 4)
    z_hi = module // 4
    z_lo = lax.rem(ex, 2)
    mate = feat + 1 - 2 * core
    ex_z = ex + 1 - 2 * z_lo
    ex_up, ex_down, ex_far = lax.rem(ex + 2, 8), lax.rem(ex + 6, 8), lax.rem(ex + 4, 8)

    def remote(src, dst, send, recv, to_ex, to_feat):
        return pltpu.make_async_remote_copy(
            src_ref=src, dst_ref=dst, send_sem=send, recv_sem=recv, device_id=(to_ex, to_feat), device_id_type=MESH
        )

    def arrived(ref, sem):
        pltpu.make_async_copy(ref, ref, sem).wait()

    own_raw = pltpu.make_async_copy(
        queries.at[:, pl.ds(pl.multiple_of(module * 4096, 4096), 4096)], raw.at[0, y], raw_recv.at[0, y]
    )
    own_raw.start()
    load_out = pltpu.make_async_copy(inv_out.at[module], factor.at[0], local_sem.at[0])
    load_in = pltpu.make_async_copy(inv_in.at[module], factor.at[1], local_sem.at[1])
    load_train = pltpu.make_async_copy(train, train_v, local_sem.at[2])
    load_out.start()
    load_in.start()

    barrier = pltpu.get_barrier_semaphore()

    for dz in range(4):
        for dy in range(4):
            if (dz, dy) != (0, 0):
                peer = (lax.rem(z_hi + dz, 4) * 4 + lax.rem(y + dy, 4)) * 2 + core
                pl.semaphore_signal(barrier, inc=1, device_id=(ex, peer), device_id_type=MESH)
    pl.semaphore_signal(barrier, inc=1, device_id=(ex, mate), device_id_type=MESH)
    for peer in (ex_z, ex_up, ex_down):
        pl.semaphore_signal(barrier, inc=1, device_id=(peer, feat), device_id_type=MESH)
    for peer in (ex_up, ex_down):
        pl.semaphore_signal(barrier, inc=1, device_id=(peer, mate), device_id_type=MESH)
    pl.semaphore_wait(barrier, 21)

    sends = []

    def send(*args):
        copy = remote(*args)
        copy.start()
        sends.append(copy)

    def send_raw(dz, dy):
        to_module = lax.rem(z_hi + 4 - dz, 4) * 4 + lax.rem(y + dy, 4)
        send(
            queries.at[:, pl.ds(pl.multiple_of(to_module * 4096, 4096), 4096)],
            raw.at[dz, y], raw_send.at[dz, dy], raw_recv.at[dz, y], ex, to_module * 2 + core,
        )

    def raw_out(dz):
        for dy in (2, 1, 3, 0):
            if (dz, dy) != (0, 0):
                send_raw(dz, dy)

    for first in (0, 1, 3,):
        raw_out(first)

    load_train.start()
    load_out.wait()
    load_in.wait()
    r_row = lax.broadcasted_iota(jnp.int32, (64, 64), 0)
    r_col = lax.broadcasted_iota(jnp.int32, (64, 64), 1)
    place = where_ones(r_row == jnp.where(r_col < 32, 2 * r_col, 2 * r_col - 63))
    place_t = where_ones(r_col == jnp.where(r_row < 32, 2 * r_row, 2 * r_row - 63))
    left = []
    for term in halves(factor[0]):
        turned = dot(term, place).astype(BF16)
        left.append(dot(place_t, turned).astype(BF16))
    tall = where_ones(
        lax.broadcasted_iota(jnp.int32, (256, 64), 0) % 64 == lax.broadcasted_iota(jnp.int32, (256, 64), 1)
    )
    wide = where_ones(
        lax.broadcasted_iota(jnp.int32, (64, 256), 1) % 64 == lax.broadcasted_iota(jnp.int32, (64, 256), 0)
    )
    same = (
        lax.broadcasted_iota(jnp.int32, (256, 256), 0) // 64 == lax.broadcasted_iota(jnp.int32, (256, 256), 1) // 64
    )
    right = []
    for term in halves(factor[1]):
        full = dot(dot(tall, term).astype(BF16), wide)
        right.append(jnp.where(same, full, 0.0).astype(BF16))
    rows = lax.broadcasted_iota(jnp.int32, (256, 256), 0) % 64
    row = jnp.where(rows < 32, 2 * rows, 2 * rows - 63)
    live = jnp.where(row < ranks[module], 1.0, 0.0).astype(F32)
    low = lax.broadcasted_iota(jnp.int32, (32, 128), 1) < 64

    def own_rows(e, start, count):
        return pl.ds(pl.multiple_of(lax.rem(e + 8 - 2 * z_hi, 8) * 32 + start, 16), count)

    def precondition(k):
        for ys in range(4):
            arrived(raw.at[k, ys], raw_recv.at[k, ys])
        for ys in range(4):
            block = raw[k, ys].astype(F32)
            for r in range(32):
                spread[ys * 128 + 4 * r : ys * 128 + 4 * r + 4, :] = block[:, r * 128 : (r + 1) * 128]
        for p in range(8):
            first = (p // 2) * 128 + 2 * (p % 2)
            a = spread[pl.ds(first, 32, stride=4), :]
            b = spread[pl.ds(first + 1, 32, stride=4), :]
            lanes = slice(p * 128, (p + 1) * 128)
            mixed_in[0:32, lanes] = jnp.where(low, a, pltpu.roll(b, 64, 1)).astype(BF16)
            mixed_in[32:64, lanes] = jnp.where(low, pltpu.roll(a, 64, 1), b).astype(BF16)
        value = mixed_in[...]
        turned = dot(left[0], value) + dot(left[1], value)
        high, rest = halves(jnp.concatenate([turned[:, g * 256 : (g + 1) * 256] for g in range(4)], axis=0))
        mixed = (dot(high, right[0]) + (dot(rest, right[0]) + dot(high, right[1]))) * live
        for p in range(8):
            g, lanes = p // 2, slice(p % 2 * 128, (p % 2 + 1) * 128)
            even = mixed[g * 64 : g * 64 + 32, lanes]
            odd = mixed[g * 64 + 32 : g * 64 + 64, lanes]
            mixed_out[64 * p : 64 * p + 32, :] = jnp.where(low, even, pltpu.roll(odd, 64, 1))
            mixed_out[64 * p + 32 : 64 * p + 64, :] = jnp.where(low, pltpu.roll(even, 64, 1), odd)
        for i in range(16):
            lanes = slice(i * 128, (i + 1) * 128)
            other[k, :, lanes] = mixed_out[pl.ds((1 - core) * 16 + i, 16, stride=32), :].astype(BF16)
        mine = own_rows(ex, core * 16, 16)
        send(other.at[k], cond.at[k, mine], mate_send.at[k], mate_recv.at[k], ex, mate)
        for i in range(16):
            lanes = slice(i * 128, (i + 1) * 128)
            cond[k, mine, lanes] = mixed_out[pl.ds(core * 16 + i, 16, stride=32), :].astype(BF16)

    def to_x(k, rows_, way, what):
        ref = cond.at[k, rows_]
        send(ref, ref, x_send.at[k, way, what], x_recv.at[k, way, what], (ex_up, ex_down)[way], feat)

    def from_x(k, rows_, way, what):
        arrived(cond.at[k, rows_], x_recv.at[k, way, what])

    def to_z(k, rows_, what):
        ref = cond.at[k, rows_]
        send(ref, ref, zlo_send.at[k, what], zlo_recv.at[k, what], ex_z, feat)

    def from_z(k, rows_, what):
        arrived(cond.at[k, rows_], zlo_recv.at[k, what])

    def first_hop(k):
        mine = own_rows(ex, core * 16, 16)
        for way, to_ex in enumerate((ex_up, ex_down)):
            arrival = first_recv.at[k, way, core]
            send(cond.at[k, mine], cond.at[k, mine], first_send.at[k, way, 0], arrival, to_ex, feat)
            send(other.at[k], cond.at[k, mine], first_send.at[k, way, 1], arrival, to_ex, mate)

    def side(k):
        to_z(k, own_rows(ex, 0, 32), 0)

    def second_hop(k):
        from_z(k, own_rows(ex_z, 0, 32), 0)
        to_x(k, own_rows(ex_z, 0, 32), 0, 1)
        to_x(k, own_rows(ex_z, 0, 32), 1, 1)

    def swap(e):
        return e + 1 - 2 * z_lo

    def forward(k, what):
        below = ex_down if what == 0 else swap(ex_down)
        above = ex_up if what == 0 else swap(ex_up)
        if what == 0:
            arrived(cond.at[k, own_rows(below, 0, 16)], first_recv.at[k, 0, 0])
        else:
            from_x(k, own_rows(below, 0, 32), 0, what)
        to_x(k, own_rows(below, 0, 16), 0, what + 2)
        if what == 0:
            arrived(cond.at[k, own_rows(above, 16, 16)], first_recv.at[k, 1, 1])
        else:
            from_x(k, own_rows(above, 0, 32), 1, what)
        to_x(k, own_rows(above, 16, 16), 1, what + 2)

    def rest(k):
        arrived(cond.at[k, own_rows(ex_down, 16, 16)], first_recv.at[k, 0, 1])
        arrived(cond.at[k, own_rows(ex_up, 0, 16)], first_recv.at[k, 1, 0])

    def near_to_z(k):
        rest(k)
        to_z(k, own_rows(ex_down, 0, 32), 1)
        to_z(k, own_rows(ex_up, 0, 32), 2)

    def far_to_z(k):
        from_x(k, own_rows(ex_far, 0, 16), 0, 2)
        to_z(k, own_rows(ex_far, 0, 16), 3)
        from_x(k, own_rows(ex_far, 16, 16), 1, 2)
        to_z(k, own_rows(ex_far, 16, 16), 4)

    def direct(k):
        for way in range(2):
            ref = cond.at[k, own_rows(ex_z, 16 * way, 16)]
            send(ref, ref, x_send.at[k, way, 3], x_recv.at[k, way, 3], ex_far, feat)

    def complete(k):
        if k not in XZ:
            rest(k)
        if k in DIRECT:
            from_x(k, own_rows(swap(ex_down), 0, 32), 0, 1)
            from_x(k, own_rows(swap(ex_up), 0, 32), 1, 1)
        if k in XZ:
            from_z(k, own_rows(ex_z, 0, 32), 0)
            from_z(k, own_rows(swap(ex_down), 0, 32), 1)
            from_z(k, own_rows(swap(ex_up), 0, 32), 2)
            from_z(k, own_rows(swap(ex_far), 0, 16), 3)
            from_z(k, own_rows(swap(ex_far), 16, 16), 4)
        else:
            for what in range(2):
                far = ex_far if what == 0 else swap(ex_far)
                from_x(k, own_rows(far, 0, 16), 0, what + 2)
                from_x(k, own_rows(far, 16, 16), 1, what + 2)

    def multiply(k, t):
        part[k, t] = dot_t(cond[k], train_v[t * TW : (t + 1) * TW, :])
        give = pl.ds(pl.multiple_of((1 - core) * 128, 128), 128)
        send(part.at[k, t, give], pair.at[k, t], pair_send.at[k, t], pair_recv.at[k, t], ex, mate)

    def block_of(y_):
        return 2 * (y_ % 2) + y_ // 2

    def summed(k, t, y_):
        at = pl.multiple_of(block_of(y_) * 32, 32)
        return part[k, t, pl.ds(pl.multiple_of(core * 128 + at, 32), 32), :] + pair[k, t, pl.ds(at, 32), :]

    def reduce_y(k, t):
        arrived(pair.at[k, t], pair_recv.at[k, t])
        for dy in (2, 1, 3):
            to_y = lax.rem(y + dy, 4)
            out_y[k, t, dy - 1] = summed(k, t, to_y).astype(BF16)
            send(
                out_y.at[k, t, dy - 1], in_y.at[k, t, dy - 1], y_send.at[k, t, dy - 1], y_recv.at[k, t, dy - 1],
                ex, (z_hi * 4 + to_y) * 2 + core,
            )

    late = []

    def reduce_z(k, t):
        total = summed(k, t, y)
        for dy in (1, 3, 2):
            arrived(in_y.at[k, t, dy - 1], y_recv.at[k, t, dy - 1])
            total = total + in_y[k, t, dy - 1].astype(F32)
        owner = 4 * lax.rem(4 * core + block_of(y) + 2 * z_hi, 8) + lax.rem(z_hi + k, 4)
        out_z[k, t] = total.astype(BF16)
        copy = remote(out_z.at[k, t], in_z.at[z_hi, t], z_send.at[k, t], z_recv.at[z_hi, t], ex, owner)
        late.append((owner, copy))

        @pl.when(owner != feat)
        def _():
            copy.start()

        @pl.when(owner == feat)
        def _():
            in_z[z_hi, t] = out_z[k, t]

    def from_mate(k):
        arrived(cond.at[k, own_rows(ex, (1 - core) * 16, 16)], mate_recv.at[k])

    precondition(0)
    first_hop(0)
    raw_out(2)
    forward(0, 0)
    from_mate(0)
    precondition(1)
    first_hop(1)
    from_mate(1)
    side(1)
    precondition(3)
    first_hop(3)
    from_mate(3)
    side(3)
    side(0)
    forward(1, 0)
    second_hop(1)
    precondition(2)
    first_hop(2)
    from_mate(2)
    side(2)
    near_to_z(0)
    far_to_z(0)
    forward(3, 0)
    forward(1, 1)
    second_hop(3)
    load_train.wait()
    complete(1)
    multiply(1, 0)
    forward(2, 0)
    forward(3, 1)
    second_hop(2)
    direct(2)
    reduce_y(1, 0)
    complete(0)
    multiply(0, 0)
    complete(3)
    multiply(3, 0)
    reduce_y(0, 0)
    reduce_y(3, 0)
    reduce_z(1, 0)
    complete(2)
    multiply(2, 0)
    reduce_z(0, 0)
    reduce_y(2, 0)
    reduce_z(3, 0)
    reduce_z(2, 0)

    mine = feat // 4
    for t in range(TS):
        total = None
        for zs in range(4):
            place_ = lax.rem(mine + 8 - 2 * zs, 8)
            sender = (zs * 4 + 2 * lax.rem(place_, 2) + lax.rem(place_ // 2, 2)) * 2 + place_ // 4

            @pl.when(sender != feat)
            def _():
                arrived(in_z.at[zs, t], z_recv.at[zs, t])

            value = in_z[zs, t].astype(F32)
            total = value if total is None else total + value
        total = total * (65536.0 ** -0.5)
        for cs in range(2):
            for ys in range(4):
                at = (ys * 2 + cs) * 4
                out[at : at + 4, t * TW : (t + 1) * TW] = total[cs * 16 + ys * 4 : cs * 16 + ys * 4 + 4, :]

    for copy in sends:
        copy.wait_send()
    for owner, copy in late:

        @pl.when(owner != feat)
        def _():
            copy.wait_send()


def on_device(train_grads, queries, inv_out, inv_in, module_rank):
    any_space = pl.BlockSpec(memory_space=pltpu.HBM)
    dma = pltpu.SemaphoreType.DMA
    result = pl.pallas_call(
        kernel,
        out_shape=jax.ShapeDtypeStruct((32, 1024), F32),
        in_specs=[any_space] * 4 + [pl.BlockSpec(memory_space=pltpu.SMEM)],
        out_specs=pl.BlockSpec(memory_space=pltpu.VMEM),
        scratch_shapes=[
            pltpu.VMEM((1024, 2048), BF16),
            pltpu.VMEM((4, 4, 4, 4096), BF16),
            pltpu.VMEM((2, 64, 64), F32),
            pltpu.VMEM((512, 128), F32),
            pltpu.VMEM((64, 1024), BF16),
            pltpu.VMEM((512, 128), F32),
            pltpu.VMEM((4, 256, 2048), BF16),
            pltpu.VMEM((4, 16, 2048), BF16),
            pltpu.VMEM((4, TS, 256, TW), F32),
            pltpu.VMEM((4, TS, 128, TW), F32),
            pltpu.VMEM((4, TS, 3, 32, TW), BF16),
            pltpu.VMEM((4, TS, 3, 32, TW), BF16),
            pltpu.VMEM((4, TS, 32, TW), BF16),
            pltpu.VMEM((4, TS, 32, TW), BF16),
            dma((3,)),
            dma((4, 4)), dma((4, 4)),
            dma((4,)), dma((4,)),
            dma((4, 5)), dma((4, 5)),
            dma((4, 2, 4)), dma((4, 2, 4)),
            dma((4, 2, 2)), dma((4, 2, 2)),
            dma((4, TS)), dma((4, TS)),
            dma((4, TS, 3)), dma((4, TS, 3)),
            dma((4, TS)), dma((4, TS)),
        ],
        compiler_params=pltpu.CompilerParams(
            collective_id=0, has_side_effects=True, vmem_limit_bytes=60 * 1024 * 1024
        ),
        cost_estimate=pl.CostEstimate(flops=2 * 1024 * 1024 * 2048, bytes_accessed=8 * 1024 * 1024, transcendentals=0),
    )(train_grads, queries, inv_out, inv_in, module_rank)
    return result.T


def solution(mesh):
    return jax.shard_map(
        on_device,
        mesh=mesh,
        in_specs=(P("ex", "feat"), P(("ex", "feat"), None), P(), P(), P()),
        out_specs=P("ex", "feat"),
        check_vma=False,
    )
```

```python
import jax
import jax.numpy as jnp
from jax import lax
from jax.experimental import pallas as pl
from jax.experimental.pallas import tpu as pltpu
from jax.sharding import PartitionSpec as P

MESH = pl.DeviceIdType.MESH
F32 = jnp.float32
BF16 = jnp.bfloat16
TS = 1
TW = 1024 // TS
XZ = (0,)
DIRECT = (2,)


def dot(a, b):
    return jnp.dot(a, b, preferred_element_type=F32)


def dot_t(a, b):
    return lax.dot_general(a, b, (((1,), (1,)), ((), ())), preferred_element_type=F32)


def halves(value):
    high = value.astype(BF16)
    return high, (value - high.astype(F32)).astype(BF16)


def where_ones(mask):
    return jnp.where(mask, 1.0, 0.0).astype(BF16)


def kernel(
    train, queries, inv_out, inv_in, ranks, out,
    train_v, near, raw, factor, spread, mixed_in, mixed_out, cond, other, part, pair, out_y, in_y, out_z, in_z,
    local_sem, raw_send, raw_recv, mate_send, mate_recv, zlo_send, zlo_recv, x_send, x_recv, first_send, first_recv,
    pair_send, pair_recv, y_send, y_recv, z_send, z_recv,
):
    ex, feat = lax.axis_index("ex"), lax.axis_index("feat")
    core = lax.rem(feat, 2)
    module = feat // 2
    y = lax.rem(module, 4)
    z_hi = module // 4
    z_lo = lax.rem(ex, 2)
    mate = feat + 1 - 2 * core
    ex_z = ex + 1 - 2 * z_lo
    ex_up, ex_down, ex_far = lax.rem(ex + 2, 8), lax.rem(ex + 6, 8), lax.rem(ex + 4, 8)

    def remote(src, dst, send, recv, to_ex, to_feat):
        return pltpu.make_async_remote_copy(
            src_ref=src, dst_ref=dst, send_sem=send, recv_sem=recv, device_id=(to_ex, to_feat), device_id_type=MESH
        )

    def arrived(ref, sem):
        pltpu.make_async_copy(ref, ref, sem).wait()

    load_queries = pltpu.make_async_copy(queries, near, local_sem.at[3])
    load_queries.start()
    own_raw = pltpu.make_async_copy(
        queries.at[:, pl.ds(pl.multiple_of(module * 4096, 4096), 4096)], raw.at[0, y], raw_recv.at[0, y]
    )
    own_raw.start()
    load_out = pltpu.make_async_copy(inv_out.at[module], factor.at[0], local_sem.at[0])
    load_in = pltpu.make_async_copy(inv_in.at[module], factor.at[1], local_sem.at[1])
    load_train = pltpu.make_async_copy(train, train_v, local_sem.at[2])
    load_out.start()
    load_in.start()

    barrier = pltpu.get_barrier_semaphore()

    for dz in range(4):
        for dy in range(4):
            if (dz, dy) != (0, 0):
                peer = (lax.rem(z_hi + dz, 4) * 4 + lax.rem(y + dy, 4)) * 2 + core
                pl.semaphore_signal(barrier, inc=1, device_id=(ex, peer), device_id_type=MESH)
    pl.semaphore_signal(barrier, inc=1, device_id=(ex, mate), device_id_type=MESH)
    for peer in (ex_z, ex_up, ex_down):
        pl.semaphore_signal(barrier, inc=1, device_id=(peer, feat), device_id_type=MESH)
    for peer in (ex_up, ex_down):
        pl.semaphore_signal(barrier, inc=1, device_id=(peer, mate), device_id_type=MESH)
    pl.semaphore_wait(barrier, 21)

    sends = []

    def send(*args):
        copy = remote(*args)
        copy.start()
        sends.append(copy)

    load_queries.wait()

    def send_raw(dz, dy):
        to_module = lax.rem(z_hi + 4 - dz, 4) * 4 + lax.rem(y + dy, 4)
        send(
            near.at[:, pl.ds(pl.multiple_of(to_module * 4096, 4096), 4096)],
            raw.at[dz, y], raw_send.at[dz, dy], raw_recv.at[dz, y], ex, to_module * 2 + core,
        )

    def raw_out(dz):
        for dy in (2, 1, 3, 0):
            if (dz, dy) != (0, 0):
                send_raw(dz, dy)

    for first in (0, 1, 3,):
        raw_out(first)

    load_train.start()
    load_out.wait()
    load_in.wait()
    r_row = lax.broadcasted_iota(jnp.int32, (64, 64), 0)
    r_col = lax.broadcasted_iota(jnp.int32, (64, 64), 1)
    place = where_ones(r_row == jnp.where(r_col < 32, 2 * r_col, 2 * r_col - 63))
    place_t = where_ones(r_col == jnp.where(r_row < 32, 2 * r_row, 2 * r_row - 63))
    left = []
    for term in halves(factor[0]):
        turned = dot(term, place).astype(BF16)
        left.append(dot(place_t, turned).astype(BF16))
    tall = where_ones(
        (lax.broadcasted_iota(jnp.int32, (256, 64), 0) & 63) == lax.broadcasted_iota(jnp.int32, (256, 64), 1)
    )
    wide = where_ones(
        (lax.broadcasted_iota(jnp.int32, (64, 256), 1) & 63) == lax.broadcasted_iota(jnp.int32, (64, 256), 0)
    )
    same = (lax.broadcasted_iota(jnp.int32, (256, 256), 0) ^ lax.broadcasted_iota(jnp.int32, (256, 256), 1)) < 64
    right = []
    for term in halves(factor[1]):
        full = dot(dot(tall, term).astype(BF16), wide)
        right.append(jnp.where(same, full, 0.0).astype(BF16))
    rows = lax.broadcasted_iota(jnp.int32, (256, 256), 0) & 63
    row = jnp.where(rows < 32, 2 * rows, 2 * rows - 63)
    live = jnp.where(row < ranks[module], 1.0, 0.0).astype(F32)
    low = lax.broadcasted_iota(jnp.int32, (32, 128), 1) < 64

    def own_rows(e, start, count):
        return pl.ds(pl.multiple_of(lax.rem(e + 8 - 2 * z_hi, 8) * 32 + start, 16), count)

    def precondition(k):
        for ys in range(4):
            arrived(raw.at[k, ys], raw_recv.at[k, ys])
        for ys in range(4):
            block = raw[k, ys].astype(F32)
            for r in range(32):
                spread[ys * 128 + 4 * r : ys * 128 + 4 * r + 4, :] = block[:, r * 128 : (r + 1) * 128]
        for p in range(8):
            first = (p // 2) * 128 + 2 * (p % 2)
            a = spread[pl.ds(first, 32, stride=4), :]
            b = spread[pl.ds(first + 1, 32, stride=4), :]
            lanes = slice(p * 128, (p + 1) * 128)
            mixed_in[0:32, lanes] = jnp.where(low, a, pltpu.roll(b, 64, 1)).astype(BF16)
            mixed_in[32:64, lanes] = jnp.where(low, pltpu.roll(a, 64, 1), b).astype(BF16)
        value = mixed_in[...]
        turned = dot(left[0], value) + dot(left[1], value)
        high, rest = halves(jnp.concatenate([turned[:, g * 256 : (g + 1) * 256] for g in range(4)], axis=0))
        mixed = (dot(high, right[0]) + (dot(rest, right[0]) + dot(high, right[1]))) * live
        for p in range(8):
            g, lanes = p // 2, slice(p % 2 * 128, (p % 2 + 1) * 128)
            even = mixed[g * 64 : g * 64 + 32, lanes]
            odd = mixed[g * 64 + 32 : g * 64 + 64, lanes]
            mixed_out[64 * p : 64 * p + 32, :] = jnp.where(low, even, pltpu.roll(odd, 64, 1))
            mixed_out[64 * p + 32 : 64 * p + 64, :] = jnp.where(low, pltpu.roll(even, 64, 1), odd)
        for i in range(16):
            lanes = slice(i * 128, (i + 1) * 128)
            other[k, :, lanes] = mixed_out[pl.ds((1 - core) * 16 + i, 16, stride=32), :].astype(BF16)
        mine = own_rows(ex, core * 16, 16)
        send(other.at[k], cond.at[k, mine], mate_send.at[k], mate_recv.at[k], ex, mate)
        for i in range(16):
            lanes = slice(i * 128, (i + 1) * 128)
            cond[k, mine, lanes] = mixed_out[pl.ds(core * 16 + i, 16, stride=32), :].astype(BF16)

    def to_x(k, rows_, way, what):
        ref = cond.at[k, rows_]
        send(ref, ref, x_send.at[k, way, what], x_recv.at[k, way, what], (ex_up, ex_down)[way], feat)

    def from_x(k, rows_, way, what):
        arrived(cond.at[k, rows_], x_recv.at[k, way, what])

    def to_z(k, rows_, what):
        ref = cond.at[k, rows_]
        send(ref, ref, zlo_send.at[k, what], zlo_recv.at[k, what], ex_z, feat)

    def from_z(k, rows_, what):
        arrived(cond.at[k, rows_], zlo_recv.at[k, what])

    def first_hop(k):
        mine = own_rows(ex, core * 16, 16)
        for way, to_ex in enumerate((ex_up, ex_down)):
            arrival = first_recv.at[k, way, core]
            send(cond.at[k, mine], cond.at[k, mine], first_send.at[k, way, 0], arrival, to_ex, feat)
            send(other.at[k], cond.at[k, mine], first_send.at[k, way, 1], arrival, to_ex, mate)

    def side(k):
        to_z(k, own_rows(ex, 0, 32), 0)

    def second_hop(k):
        from_z(k, own_rows(ex_z, 0, 32), 0)
        to_x(k, own_rows(ex_z, 0, 32), 0, 1)
        to_x(k, own_rows(ex_z, 0, 32), 1, 1)

    def swap(e):
        return e + 1 - 2 * z_lo

    def forward(k, what):
        below = ex_down if what == 0 else swap(ex_down)
        above = ex_up if what == 0 else swap(ex_up)
        if what == 0:
            arrived(cond.at[k, own_rows(below, 0, 16)], first_recv.at[k, 0, 0])
        else:
            from_x(k, own_rows(below, 0, 32), 0, what)
        to_x(k, own_rows(below, 0, 16), 0, what + 2)
        if what == 0:
            arrived(cond.at[k, own_rows(above, 16, 16)], first_recv.at[k, 1, 1])
        else:
            from_x(k, own_rows(above, 0, 32), 1, what)
        to_x(k, own_rows(above, 16, 16), 1, what + 2)

    def rest(k):
        arrived(cond.at[k, own_rows(ex_down, 16, 16)], first_recv.at[k, 0, 1])
        arrived(cond.at[k, own_rows(ex_up, 0, 16)], first_recv.at[k, 1, 0])

    def near_to_z(k):
        rest(k)
        to_z(k, own_rows(ex_down, 0, 32), 1)
        to_z(k, own_rows(ex_up, 0, 32), 2)

    def far_to_z(k):
        from_x(k, own_rows(ex_far, 0, 16), 0, 2)
        to_z(k, own_rows(ex_far, 0, 16), 3)
        from_x(k, own_rows(ex_far, 16, 16), 1, 2)
        to_z(k, own_rows(ex_far, 16, 16), 4)

    def direct(k):
        for way in range(2):
            ref = cond.at[k, own_rows(ex_z, 16 * way, 16)]
            send(ref, ref, x_send.at[k, way, 3], x_recv.at[k, way, 3], ex_far, feat)

    def complete(k):
        if k not in XZ:
            rest(k)
        if k in DIRECT:
            from_x(k, own_rows(swap(ex_down), 0, 32), 0, 1)
            from_x(k, own_rows(swap(ex_up), 0, 32), 1, 1)
        if k in XZ:
            from_z(k, own_rows(ex_z, 0, 32), 0)
            from_z(k, own_rows(swap(ex_down), 0, 32), 1)
            from_z(k, own_rows(swap(ex_up), 0, 32), 2)
            from_z(k, own_rows(swap(ex_far), 0, 16), 3)
            from_z(k, own_rows(swap(ex_far), 16, 16), 4)
        else:
            for what in range(2):
                far = ex_far if what == 0 else swap(ex_far)
                from_x(k, own_rows(far, 0, 16), 0, what + 2)
                from_x(k, own_rows(far, 16, 16), 1, what + 2)

    def multiply(k, t):
        part[k, t] = dot_t(cond[k], train_v[t * TW : (t + 1) * TW, :])
        give = pl.ds(pl.multiple_of((1 - core) * 128, 128), 128)
        send(part.at[k, t, give], pair.at[k, t], pair_send.at[k, t], pair_recv.at[k, t], ex, mate)

    def block_of(y_):
        return 2 * (y_ % 2) + y_ // 2

    def summed(k, t, y_):
        at = pl.multiple_of(block_of(y_) * 32, 32)
        return part[k, t, pl.ds(pl.multiple_of(core * 128 + at, 32), 32), :] + pair[k, t, pl.ds(at, 32), :]

    def reduce_y(k, t):
        arrived(pair.at[k, t], pair_recv.at[k, t])
        for dy in (2, 1, 3):
            to_y = lax.rem(y + dy, 4)
            out_y[k, t, dy - 1] = summed(k, t, to_y).astype(BF16)
            send(
                out_y.at[k, t, dy - 1], in_y.at[k, t, dy - 1], y_send.at[k, t, dy - 1], y_recv.at[k, t, dy - 1],
                ex, (z_hi * 4 + to_y) * 2 + core,
            )

    late = []

    def reduce_z(k, t):
        total = summed(k, t, y)
        for dy in (1, 3, 2):
            arrived(in_y.at[k, t, dy - 1], y_recv.at[k, t, dy - 1])
            total = total + in_y[k, t, dy - 1].astype(F32)
        owner = 4 * lax.rem(4 * core + block_of(y) + 2 * z_hi, 8) + lax.rem(z_hi + k, 4)
        out_z[k, t] = total.astype(BF16)
        copy = remote(out_z.at[k, t], in_z.at[z_hi, t], z_send.at[k, t], z_recv.at[z_hi, t], ex, owner)
        late.append((owner, copy))

        @pl.when(owner != feat)
        def _():
            copy.start()

        @pl.when(owner == feat)
        def _():
            in_z[z_hi, t] = out_z[k, t]

    def from_mate(k):
        arrived(cond.at[k, own_rows(ex, (1 - core) * 16, 16)], mate_recv.at[k])

    precondition(0)
    first_hop(0)
    raw_out(2)
    forward(0, 0)
    from_mate(0)
    precondition(1)
    first_hop(1)
    from_mate(1)
    side(1)
    precondition(3)
    first_hop(3)
    from_mate(3)
    side(3)
    forward(1, 0)
    second_hop(1)
    precondition(2)
    from_mate(2)
    side(2)
    side(0)
    near_to_z(0)
    far_to_z(0)
    forward(3, 0)
    forward(1, 1)
    second_hop(3)
    first_hop(2)
    load_train.wait()
    complete(1)
    multiply(1, 0)
    forward(3, 1)
    forward(2, 0)
    second_hop(2)
    direct(2)
    reduce_y(1, 0)
    complete(0)
    multiply(0, 0)
    reduce_y(0, 0)
    complete(3)
    multiply(3, 0)
    reduce_z(1, 0)
    reduce_y(3, 0)
    complete(2)
    multiply(2, 0)
    reduce_z(0, 0)
    reduce_y(2, 0)
    reduce_z(3, 0)
    reduce_z(2, 0)

    mine = feat // 4
    for t in range(TS):
        total = None
        for zs in range(4):
            place_ = lax.rem(mine + 8 - 2 * zs, 8)
            sender = (zs * 4 + 2 * lax.rem(place_, 2) + lax.rem(place_ // 2, 2)) * 2 + place_ // 4

            @pl.when(sender != feat)
            def _():
                arrived(in_z.at[zs, t], z_recv.at[zs, t])

            value = in_z[zs, t].astype(F32)
            total = value if total is None else total + value
        total = total * (65536.0 ** -0.5)
        for cs in range(2):
            for ys in range(4):
                at = (ys * 2 + cs) * 4
                out[at : at + 4, t * TW : (t + 1) * TW] = total[cs * 16 + ys * 4 : cs * 16 + ys * 4 + 4, :]

    for copy in sends:
        copy.wait_send()
    for owner, copy in late:

        @pl.when(owner != feat)
        def _():
            copy.wait_send()


def on_device(train_grads, queries, inv_out, inv_in, module_rank):
    any_space = pl.BlockSpec(memory_space=pltpu.HBM)
    dma = pltpu.SemaphoreType.DMA
    result = pl.pallas_call(
        kernel,
        out_shape=jax.ShapeDtypeStruct((32, 1024), F32),
        in_specs=[any_space] * 4 + [pl.BlockSpec(memory_space=pltpu.SMEM)],
        out_specs=pl.BlockSpec(memory_space=pltpu.VMEM),
        scratch_shapes=[
            pltpu.VMEM((1024, 2048), BF16),
            pltpu.VMEM((4, 65536), BF16),
            pltpu.VMEM((4, 4, 4, 4096), BF16),
            pltpu.VMEM((2, 64, 64), F32),
            pltpu.VMEM((512, 128), F32),
            pltpu.VMEM((64, 1024), BF16),
            pltpu.VMEM((512, 128), F32),
            pltpu.VMEM((4, 256, 2048), BF16),
            pltpu.VMEM((4, 16, 2048), BF16),
            pltpu.VMEM((4, TS, 256, TW), F32),
            pltpu.VMEM((4, TS, 128, TW), F32),
            pltpu.VMEM((4, TS, 3, 32, TW), BF16),
            pltpu.VMEM((4, TS, 3, 32, TW), BF16),
            pltpu.VMEM((4, TS, 32, TW), BF16),
            pltpu.VMEM((4, TS, 32, TW), BF16),
            dma((4,)),
            dma((4, 4)), dma((4, 4)),
            dma((4,)), dma((4,)),
            dma((4, 5)), dma((4, 5)),
            dma((4, 2, 4)), dma((4, 2, 4)),
            dma((4, 2, 2)), dma((4, 2, 2)),
            dma((4, TS)), dma((4, TS)),
            dma((4, TS, 3)), dma((4, TS, 3)),
            dma((4, TS)), dma((4, TS)),
        ],
        compiler_params=pltpu.CompilerParams(
            collective_id=0, has_side_effects=True, vmem_limit_bytes=60 * 1024 * 1024
        ),
        cost_estimate=pl.CostEstimate(flops=2 * 1024 * 1024 * 2048, bytes_accessed=8 * 1024 * 1024, transcendentals=0),
    )(train_grads, queries, inv_out, inv_in, module_rank)
    return result.T


def solution(mesh):
    return jax.shard_map(
        on_device,
        mesh=mesh,
        in_specs=(P("ex", "feat"), P(("ex", "feat"), None), P(), P(), P()),
        out_specs=P("ex", "feat"),
        check_vma=False,
    )
```

```python
import jax
import jax.numpy as jnp
from jax import lax
from jax.experimental import pallas as pl
from jax.experimental.pallas import tpu as pltpu
from jax.sharding import PartitionSpec as P

MESH = pl.DeviceIdType.MESH
F32 = jnp.float32
BF16 = jnp.bfloat16
TS = 1
TW = 1024 // TS
XZ = (0,)
DIRECT = (2,)


def dot(a, b):
    return jnp.dot(a, b, preferred_element_type=F32)


def dot_t(a, b):
    return lax.dot_general(a, b, (((1,), (1,)), ((), ())), preferred_element_type=F32)


def halves(value):
    high = value.astype(BF16)
    return high, (value - high.astype(F32)).astype(BF16)


def where_ones(mask):
    return jnp.where(mask, 1.0, 0.0).astype(BF16)


def kernel(
    train, queries, inv_out, inv_in, ranks, out,
    train_v, near, raw, factor, spread, mixed_in, mixed_out, cond, other, part, pair, out_y, in_y, out_z, in_z,
    local_sem, raw_send, raw_recv, mate_send, mate_recv, zlo_send, zlo_recv, x_send, x_recv, first_send, first_recv,
    pair_send, pair_recv, y_send, y_recv, z_send, z_recv,
):
    ex, feat = lax.axis_index("ex"), lax.axis_index("feat")
    core = lax.rem(feat, 2)
    module = feat // 2
    y = lax.rem(module, 4)
    z_hi = module // 4
    z_lo = lax.rem(ex, 2)
    mate = feat + 1 - 2 * core
    ex_z = ex + 1 - 2 * z_lo
    ex_up, ex_down, ex_far = lax.rem(ex + 2, 8), lax.rem(ex + 6, 8), lax.rem(ex + 4, 8)

    def remote(src, dst, send, recv, to_ex, to_feat):
        return pltpu.make_async_remote_copy(
            src_ref=src, dst_ref=dst, send_sem=send, recv_sem=recv, device_id=(to_ex, to_feat), device_id_type=MESH
        )

    def arrived(ref, sem):
        pltpu.make_async_copy(ref, ref, sem).wait()

    load_queries = pltpu.make_async_copy(queries, near, local_sem.at[3])
    load_queries.start()
    own_raw = pltpu.make_async_copy(
        queries.at[:, pl.ds(pl.multiple_of(module * 4096, 4096), 4096)], raw.at[0, y], raw_recv.at[0, y]
    )
    own_raw.start()
    load_out = pltpu.make_async_copy(inv_out.at[module], factor.at[0], local_sem.at[0])
    load_in = pltpu.make_async_copy(inv_in.at[module], factor.at[1], local_sem.at[1])
    load_train = pltpu.make_async_copy(train, train_v, local_sem.at[2])
    load_out.start()
    load_in.start()

    barrier = pltpu.get_barrier_semaphore()

    for dz in range(4):
        for dy in range(4):
            if (dz, dy) != (0, 0) and (dz != 2 or dy == 0):
                peer = (lax.rem(z_hi + dz, 4) * 4 + lax.rem(y + dy, 4)) * 2 + core
                pl.semaphore_signal(barrier, inc=1, device_id=(ex, peer), device_id_type=MESH)
    pl.semaphore_signal(barrier, inc=1, device_id=(ex, mate), device_id_type=MESH)
    for peer in (ex_z, ex_up, ex_down):
        pl.semaphore_signal(barrier, inc=1, device_id=(peer, feat), device_id_type=MESH)
    for peer in (ex_up, ex_down):
        pl.semaphore_signal(barrier, inc=1, device_id=(peer, mate), device_id_type=MESH)
    pl.semaphore_wait(barrier, 18)

    sends = []

    def send(*args):
        copy = remote(*args)
        copy.start()
        sends.append(copy)

    load_queries.wait()

    def send_raw(dz, dy):
        to_module = lax.rem(z_hi + 4 - dz, 4) * 4 + lax.rem(y + dy, 4)
        send(
            near.at[:, pl.ds(pl.multiple_of(to_module * 4096, 4096), 4096)],
            raw.at[dz, y], raw_send.at[dz, dy], raw_recv.at[dz, y], ex, to_module * 2 + core,
        )

    def raw_out(dz):
        for dy in (2, 1, 3, 0):
            if (dz, dy) != (0, 0):
                send_raw(dz, dy)

    for first in (0, 1, 3,):
        raw_out(first)

    load_train.start()
    load_out.wait()
    load_in.wait()
    r_row = lax.broadcasted_iota(jnp.int32, (64, 64), 0)
    r_col = lax.broadcasted_iota(jnp.int32, (64, 64), 1)
    place = where_ones(r_row == jnp.where(r_col < 32, 2 * r_col, 2 * r_col - 63))
    place_t = where_ones(r_col == jnp.where(r_row < 32, 2 * r_row, 2 * r_row - 63))
    left = []
    for term in halves(factor[0]):
        turned = dot(term, place).astype(BF16)
        left.append(dot(place_t, turned).astype(BF16))
    tall = where_ones(
        (lax.broadcasted_iota(jnp.int32, (256, 64), 0) & 63) == lax.broadcasted_iota(jnp.int32, (256, 64), 1)
    )
    wide = where_ones(
        (lax.broadcasted_iota(jnp.int32, (64, 256), 1) & 63) == lax.broadcasted_iota(jnp.int32, (64, 256), 0)
    )
    same = (lax.broadcasted_iota(jnp.int32, (256, 256), 0) ^ lax.broadcasted_iota(jnp.int32, (256, 256), 1)) < 64
    right = []
    for term in halves(factor[1]):
        full = dot(dot(tall, term).astype(BF16), wide)
        right.append(jnp.where(same, full, 0.0).astype(BF16))
    rows = lax.broadcasted_iota(jnp.int32, (256, 256), 0) & 63
    row = jnp.where(rows < 32, 2 * rows, 2 * rows - 63)
    live = jnp.where(row < ranks[module], 1.0, 0.0).astype(F32)
    low = lax.broadcasted_iota(jnp.int32, (32, 128), 1) < 64

    def own_rows(e, start, count):
        return pl.ds(pl.multiple_of(lax.rem(e + 8 - 2 * z_hi, 8) * 32 + start, 16), count)

    def precondition(k):
        for ys in range(4):
            arrived(raw.at[k, ys], raw_recv.at[k, ys])
        for ys in range(4):
            block = raw[k, ys].astype(F32)
            for r in range(32):
                spread[ys * 128 + 4 * r : ys * 128 + 4 * r + 4, :] = block[:, r * 128 : (r + 1) * 128]
        for p in range(8):
            first = (p // 2) * 128 + 2 * (p % 2)
            a = spread[pl.ds(first, 32, stride=4), :]
            b = spread[pl.ds(first + 1, 32, stride=4), :]
            lanes = slice(p * 128, (p + 1) * 128)
            mixed_in[0:32, lanes] = jnp.where(low, a, pltpu.roll(b, 64, 1)).astype(BF16)
            mixed_in[32:64, lanes] = jnp.where(low, pltpu.roll(a, 64, 1), b).astype(BF16)
        value = mixed_in[...]
        turned = dot(left[0], value) + dot(left[1], value)
        high, rest = halves(jnp.concatenate([turned[:, g * 256 : (g + 1) * 256] for g in range(4)], axis=0))
        mixed = (dot(high, right[0]) + (dot(rest, right[0]) + dot(high, right[1]))) * live
        for p in range(8):
            g, lanes = p // 2, slice(p % 2 * 128, (p % 2 + 1) * 128)
            even = mixed[g * 64 : g * 64 + 32, lanes]
            odd = mixed[g * 64 + 32 : g * 64 + 64, lanes]
            mixed_out[64 * p : 64 * p + 32, :] = jnp.where(low, even, pltpu.roll(odd, 64, 1))
            mixed_out[64 * p + 32 : 64 * p + 64, :] = jnp.where(low, pltpu.roll(even, 64, 1), odd)
        for i in range(16):
            lanes = slice(i * 128, (i + 1) * 128)
            other[k, :, lanes] = mixed_out[pl.ds((1 - core) * 16 + i, 16, stride=32), :].astype(BF16)
        mine = own_rows(ex, core * 16, 16)
        send(other.at[k], cond.at[k, mine], mate_send.at[k], mate_recv.at[k], ex, mate)
        for i in range(16):
            lanes = slice(i * 128, (i + 1) * 128)
            cond[k, mine, lanes] = mixed_out[pl.ds(core * 16 + i, 16, stride=32), :].astype(BF16)

    def to_x(k, rows_, way, what):
        ref = cond.at[k, rows_]
        send(ref, ref, x_send.at[k, way, what], x_recv.at[k, way, what], (ex_up, ex_down)[way], feat)

    def from_x(k, rows_, way, what):
        arrived(cond.at[k, rows_], x_recv.at[k, way, what])

    def to_z(k, rows_, what):
        ref = cond.at[k, rows_]
        send(ref, ref, zlo_send.at[k, what], zlo_recv.at[k, what], ex_z, feat)

    def from_z(k, rows_, what):
        arrived(cond.at[k, rows_], zlo_recv.at[k, what])

    def first_hop(k):
        mine = own_rows(ex, core * 16, 16)
        for way, to_ex in enumerate((ex_up, ex_down)):
            arrival = first_recv.at[k, way, core]
            send(cond.at[k, mine], cond.at[k, mine], first_send.at[k, way, 0], arrival, to_ex, feat)
            send(other.at[k], cond.at[k, mine], first_send.at[k, way, 1], arrival, to_ex, mate)

    def side(k):
        to_z(k, own_rows(ex, 0, 32), 0)

    def second_hop(k):
        from_z(k, own_rows(ex_z, 0, 32), 0)
        to_x(k, own_rows(ex_z, 0, 32), 0, 1)
        to_x(k, own_rows(ex_z, 0, 32), 1, 1)

    def swap(e):
        return e + 1 - 2 * z_lo

    def forward(k, what):
        below = ex_down if what == 0 else swap(ex_down)
        above = ex_up if what == 0 else swap(ex_up)
        if what == 0:
            arrived(cond.at[k, own_rows(below, 0, 16)], first_recv.at[k, 0, 0])
        else:
            from_x(k, own_rows(below, 0, 32), 0, what)
        to_x(k, own_rows(below, 0, 16), 0, what + 2)
        if what == 0:
            arrived(cond.at[k, own_rows(above, 16, 16)], first_recv.at[k, 1, 1])
        else:
            from_x(k, own_rows(above, 0, 32), 1, what)
        to_x(k, own_rows(above, 16, 16), 1, what + 2)

    def rest(k):
        arrived(cond.at[k, own_rows(ex_down, 16, 16)], first_recv.at[k, 0, 1])
        arrived(cond.at[k, own_rows(ex_up, 0, 16)], first_recv.at[k, 1, 0])

    def near_to_z(k):
        rest(k)
        to_z(k, own_rows(ex_down, 0, 32), 1)
        to_z(k, own_rows(ex_up, 0, 32), 2)

    def far_to_z(k):
        from_x(k, own_rows(ex_far, 0, 16), 0, 2)
        to_z(k, own_rows(ex_far, 0, 16), 3)
        from_x(k, own_rows(ex_far, 16, 16), 1, 2)
        to_z(k, own_rows(ex_far, 16, 16), 4)

    def direct(k):
        for way in range(2):
            ref = cond.at[k, own_rows(ex_z, 16 * way, 16)]
            send(ref, ref, x_send.at[k, way, 3], x_recv.at[k, way, 3], ex_far, feat)

    def complete(k):
        if k not in XZ:
            rest(k)
        if k in DIRECT:
            from_x(k, own_rows(swap(ex_down), 0, 32), 0, 1)
            from_x(k, own_rows(swap(ex_up), 0, 32), 1, 1)
        if k in XZ:
            from_z(k, own_rows(ex_z, 0, 32), 0)
            from_z(k, own_rows(swap(ex_down), 0, 32), 1)
            from_z(k, own_rows(swap(ex_up), 0, 32), 2)
            from_z(k, own_rows(swap(ex_far), 0, 16), 3)
            from_z(k, own_rows(swap(ex_far), 16, 16), 4)
        else:
            for what in range(2):
                far = ex_far if what == 0 else swap(ex_far)
                from_x(k, own_rows(far, 0, 16), 0, what + 2)
                from_x(k, own_rows(far, 16, 16), 1, what + 2)

    def multiply(k, t):
        part[k, t] = dot_t(cond[k], train_v[t * TW : (t + 1) * TW, :])
        give = pl.ds(pl.multiple_of((1 - core) * 128, 128), 128)
        send(part.at[k, t, give], pair.at[k, t], pair_send.at[k, t], pair_recv.at[k, t], ex, mate)

    def block_of(y_):
        return 2 * (y_ % 2) + y_ // 2

    def summed(k, t, y_):
        at = pl.multiple_of(block_of(y_) * 32, 32)
        return part[k, t, pl.ds(pl.multiple_of(core * 128 + at, 32), 32), :] + pair[k, t, pl.ds(at, 32), :]

    def reduce_y(k, t):
        arrived(pair.at[k, t], pair_recv.at[k, t])
        for dy in (2, 1, 3):
            to_y = lax.rem(y + dy, 4)
            out_y[k, t, dy - 1] = summed(k, t, to_y).astype(BF16)
            send(
                out_y.at[k, t, dy - 1], in_y.at[k, t, dy - 1], y_send.at[k, t, dy - 1], y_recv.at[k, t, dy - 1],
                ex, (z_hi * 4 + to_y) * 2 + core,
            )

    late = []

    def reduce_z(k, t):
        total = summed(k, t, y)
        for dy in (1, 3, 2):
            arrived(in_y.at[k, t, dy - 1], y_recv.at[k, t, dy - 1])
            total = total + in_y[k, t, dy - 1].astype(F32)
        owner = 4 * lax.rem(4 * core + block_of(y) + 2 * z_hi, 8) + lax.rem(z_hi + k, 4)
        out_z[k, t] = total.astype(BF16)
        copy = remote(out_z.at[k, t], in_z.at[z_hi, t], z_send.at[k, t], z_recv.at[z_hi, t], ex, owner)
        late.append((owner, copy))

        @pl.when(owner != feat)
        def _():
            copy.start()

        @pl.when(owner == feat)
        def _():
            in_z[z_hi, t] = out_z[k, t]

    def from_mate(k):
        arrived(cond.at[k, own_rows(ex, (1 - core) * 16, 16)], mate_recv.at[k])

    precondition(0)
    first_hop(0)
    raw_out(2)
    forward(0, 0)
    from_mate(0)
    precondition(1)
    first_hop(1)
    from_mate(1)
    side(1)
    precondition(3)
    first_hop(3)
    from_mate(3)
    side(3)
    forward(1, 0)
    second_hop(1)
    precondition(2)
    from_mate(2)
    side(2)
    side(0)
    near_to_z(0)
    far_to_z(0)
    forward(3, 0)
    forward(1, 1)
    second_hop(3)
    first_hop(2)
    load_train.wait()
    complete(1)
    multiply(1, 0)
    forward(3, 1)
    forward(2, 0)
    second_hop(2)
    direct(2)
    reduce_y(1, 0)
    complete(0)
    multiply(0, 0)
    reduce_y(0, 0)
    complete(3)
    multiply(3, 0)
    reduce_z(1, 0)
    reduce_y(3, 0)
    complete(2)
    multiply(2, 0)
    reduce_z(0, 0)
    reduce_y(2, 0)
    reduce_z(3, 0)
    reduce_z(2, 0)

    mine = feat // 4
    for t in range(TS):
        total = None
        for zs in range(4):
            place_ = lax.rem(mine + 8 - 2 * zs, 8)
            sender = (zs * 4 + 2 * lax.rem(place_, 2) + lax.rem(place_ // 2, 2)) * 2 + place_ // 4

            @pl.when(sender != feat)
            def _():
                arrived(in_z.at[zs, t], z_recv.at[zs, t])

            value = in_z[zs, t].astype(F32)
            total = value if total is None else total + value
        total = total * (65536.0 ** -0.5)
        for cs in range(2):
            for ys in range(4):
                at = (ys * 2 + cs) * 4
                out[at : at + 4, t * TW : (t + 1) * TW] = total[cs * 16 + ys * 4 : cs * 16 + ys * 4 + 4, :]

    for copy in sends:
        copy.wait_send()
    for owner, copy in late:

        @pl.when(owner != feat)
        def _():
            copy.wait_send()


def on_device(train_grads, queries, inv_out, inv_in, module_rank):
    any_space = pl.BlockSpec(memory_space=pltpu.HBM)
    dma = pltpu.SemaphoreType.DMA
    result = pl.pallas_call(
        kernel,
        out_shape=jax.ShapeDtypeStruct((32, 1024), F32),
        in_specs=[any_space] * 4 + [pl.BlockSpec(memory_space=pltpu.SMEM)],
        out_specs=pl.BlockSpec(memory_space=pltpu.VMEM),
        scratch_shapes=[
            pltpu.VMEM((1024, 2048), BF16),
            pltpu.VMEM((4, 65536), BF16),
            pltpu.VMEM((4, 4, 4, 4096), BF16),
            pltpu.VMEM((2, 64, 64), F32),
            pltpu.VMEM((512, 128), F32),
            pltpu.VMEM((64, 1024), BF16),
            pltpu.VMEM((512, 128), F32),
            pltpu.VMEM((4, 256, 2048), BF16),
            pltpu.VMEM((4, 16, 2048), BF16),
            pltpu.VMEM((4, TS, 256, TW), F32),
            pltpu.VMEM((4, TS, 128, TW), F32),
            pltpu.VMEM((4, TS, 3, 32, TW), BF16),
            pltpu.VMEM((4, TS, 3, 32, TW), BF16),
            pltpu.VMEM((4, TS, 32, TW), BF16),
            pltpu.VMEM((4, TS, 32, TW), BF16),
            dma((4,)),
            dma((4, 4)), dma((4, 4)),
            dma((4,)), dma((4,)),
            dma((4, 5)), dma((4, 5)),
            dma((4, 2, 4)), dma((4, 2, 4)),
            dma((4, 2, 2)), dma((4, 2, 2)),
            dma((4, TS)), dma((4, TS)),
            dma((4, TS, 3)), dma((4, TS, 3)),
            dma((4, TS)), dma((4, TS)),
        ],
        compiler_params=pltpu.CompilerParams(
            collective_id=0, has_side_effects=True, vmem_limit_bytes=60 * 1024 * 1024
        ),
        cost_estimate=pl.CostEstimate(flops=2 * 1024 * 1024 * 2048, bytes_accessed=8 * 1024 * 1024, transcendentals=0),
    )(train_grads, queries, inv_out, inv_in, module_rank)
    return result.T


def solution(mesh):
    return jax.shard_map(
        on_device,
        mesh=mesh,
        in_specs=(P("ex", "feat"), P(("ex", "feat"), None), P(), P(), P()),
        out_specs=P("ex", "feat"),
        check_vma=False,
    )
```
